32 devices in a mesh: sta: 8 (over z, y), tile: 4 (over x, core).
Axes of the slice: x: 2, y: 2, z: 4, core: 2. Of those that a mesh axis runs over, the one named last changes fastest.
Arguments:
- traces: bfloat16 [1536, 1536], P('sta', 'tile'), may hold values from -6 to 6
- fir_taps: float32 [4, 64], replicated, may hold values from -0.75 to 0.75
- band_gain: float32 [4], replicated, may hold values from 0.5 to 2
- starts: int32 [1536, 4], P('sta'), may hold values from 0 to 1152
- delays: int32 [1536, 8192], P('sta', 'tile'), may hold values from 0 to 127
- visibility: int32 [1536, 4], P('sta'), may hold values from 0 to 1, as said below
Outputs:
- image: float32 [8192, 256], P(('tile', 'sta'))
The draws below stay inside these ranges and needn't reach their ends.
Inputs may be any that keep to these rules, and one draw needn't show every extreme that they name: `visibility`: 1 where the station contributes to the tile's grid points, else 0; how many stations a tile uses may differ from tile to tile.
All inputs are finite; a program needn't handle non-finite values.
Results may differ from the reference program's by a relative error of at most 0.0051.
Values may be sent and summed in bfloat16 or wider, within the bound.
A program may use at most 64 MiB of HBM per device.

```python
import math
import jax
import jax.numpy as jnp
from jax import lax

BANDS = 4
TAPS = 64
D = 128
L = 256
G_DEV = 2048
WLEN = 384
TILES = 4
STATIONS = 1536
GRID = 8192
SAMP = 1536


def draw_visibility(key, part):
    first_key, second_key = jax.random.split(jax.random.fold_in(key, 7))
    level = jax.random.randint(first_key, (1, TILES), 1, 5)
    roll = jax.random.randint(second_key, (STATIONS, TILES), 0, 4)
    return (roll < level).astype(jnp.int32)


def plant(values, key, least, high):
    longest = values.shape.index(max(values.shape))
    spots = []
    for shift in (0, 1):
        where = [jax.random.randint(jax.random.fold_in(key, axis), (), 0, length) for axis, length in enumerate(values.shape)]
        where[longest] = (where[longest] + shift) % values.shape[longest]
        spots.append(tuple(where))
    return values.at[spots[0]].set(least).at[spots[1]].set(high)


def level_of(key, dims, pieces, smallest, high):
    def one(position, parts):
        draws = jax.random.uniform(jax.random.fold_in(jax.random.fold_in(key, 6), position), (parts,), jnp.float32, smallest / len(pieces), high / len(pieces))
        return jnp.repeat(jnp.exp(draws), dims[position] // parts).reshape((-1,) + (1,) * (len(dims) - position - 1))

    level = one(*pieces[0])
    for cut in pieces[1:]:
        level = level * one(*cut)
    return level


def noise(stream_key, shape, spread, bound, shards=(), kind=jnp.bfloat16):
    result = jax.random.normal(stream_key, shape, jnp.float32) * spread
    if len(shards) > 0:
        result = level_of(stream_key, shape, shards, -0.22, 0.18) * result
    return jnp.clip(result, min=-bound, max=bound).astype(kind)


def setup_inputs(seed: int = 0) -> dict:
    key_of = jax.random.split(jax.random.key(seed), 7)
    traces = noise(key_of[0], (STATIONS, SAMP), 1.0, 6.0, ((0, 8), (1, 4)))
    fir_taps = noise(key_of[1], (BANDS, TAPS), TAPS ** -0.5, 0.75, (), jnp.float32)
    band_gain = jnp.clip(jnp.exp(jax.random.uniform(key_of[2], (BANDS,), jnp.float32, math.log(0.5), math.log(2.0))), 0.5, 2.0)
    starts = plant(jax.random.randint(key_of[3], (STATIONS, TILES), 0, SAMP - WLEN + 1), jax.random.fold_in(key_of[3], 1), 0, SAMP - WLEN).astype(jnp.int32)
    delays = plant(jax.random.randint(key_of[4], (STATIONS, GRID), 0, D), jax.random.fold_in(key_of[4], 1), 0, D - 1).astype(jnp.int32)
    visibility = draw_visibility(jax.random.fold_in(key_of[6], 71), 0)
    return dict(traces=traces, fir_taps=fir_taps, band_gain=band_gain, starts=starts, delays=delays, visibility=visibility)


def band_filter(extended, fir_taps):
    signal = extended[:, None, :]
    kernel = jnp.flip(fir_taps, 1)[:, None, :]
    return lax.conv_general_dilated(signal, kernel, (1,), 'VALID', dimension_numbers=('NCH', 'OIH', 'NCH'), precision=lax.Precision.HIGHEST)

def character(extended, fir_taps, band_gain):
    filtered = band_filter(extended, fir_taps)
    return lax.optimization_barrier(jnp.sum(filtered * filtered * band_gain[None, :, None], axis=1))

def reference(traces, fir_taps, band_gain, starts, delays, visibility):
    extended = jnp.pad(traces.astype(jnp.float32), ((0, 0), (TAPS - 1, 0)))
    char_fn = character(extended, fir_taps, band_gain).astype(jnp.bfloat16)
    offsets = jnp.arange(WLEN, dtype=jnp.int32)
    sample_idx = starts[:, :, None] + offsets[None, None, :]
    raw_windows = jax.vmap(lambda trace_row, index_set: trace_row[index_set])(char_fn, sample_idx).astype(jnp.float32)
    centred = raw_windows - lax.optimization_barrier(jnp.mean(raw_windows, axis=2, keepdims=True))
    windows = (centred * visibility[:, :, None].astype(jnp.float32)).astype(jnp.bfloat16)
    lag_idx = jnp.arange(D, dtype=jnp.int32)[:, None] + jnp.arange(L, dtype=jnp.int32)[None, :]
    tile_of = jnp.arange(GRID, dtype=jnp.int32) // G_DEV

    def stack_one(total, payload):
        window, delay_row = payload
        hankel = window[:, lag_idx].reshape(TILES * D, L)
        picked_rows = hankel[tile_of * D + delay_row]
        return (total + picked_rows.astype(jnp.float32), None)
    total, unused = lax.scan(stack_one, jnp.zeros((GRID, L), jnp.float32), (windows, delays))
    return total / math.sqrt(STATIONS)
```

```python
import functools
import math

import jax
import jax.numpy as jnp
from jax import lax
from jax.experimental import pallas as pl
from jax.experimental.pallas import tpu as pltpu
from jax.sharding import PartitionSpec as P

TAPS = 64
D = 128
L = 256
WLEN = 384
LANES = 128
CHUNK = 8
MESH = pl.DeviceIdType.MESH


def window_kernel(starts_ref, gain_ref, traces_ref, taps_ref, vis_ref, win_ref, padded, held):
    sta, samp = traces_ref.shape
    bands = taps_ref.shape[0]
    padded[:, :LANES] = jnp.zeros((sta, LANES), jnp.float32)
    padded[:, LANES + samp :] = jnp.zeros((sta, LANES), jnp.float32)
    padded[:, LANES : LANES + samp] = traces_ref[...].astype(jnp.float32)

    def take(i, carry):
        for k in range(CHUNK):
            s = i * CHUNK + k
            first = starts_ref[s] + (LANES - TAPS)
            whole = first // LANES
            row = padded[pl.ds(s, 1), pl.ds(pl.multiple_of(whole * LANES, LANES), 5 * LANES)]
            row = pltpu.roll(row, 5 * LANES - (first - whole * LANES), 1)
            held[pl.ds(s, 1), :] = row[:, : 4 * LANES]
        return carry

    lax.fori_loop(0, sta // CHUNK, take, 0)

    tables = []
    for b in range(bands):
        rows = jnp.broadcast_to(taps_ref[b : b + 1, :], (2 * LANES, 2 * LANES))
        table = pltpu.roll(rows, 0, 1, stride=1, stride_axis=0)[:, :LANES]
        high = table.astype(jnp.bfloat16)
        rest = table - high.astype(jnp.float32)
        mid = rest.astype(jnp.bfloat16)
        low = (rest - mid.astype(jnp.float32)).astype(jnp.bfloat16)
        tables.append((high, mid, low))
    parts = []
    for j in range(WLEN // LANES):
        x = held[:, j * LANES : (j + 2) * LANES].astype(jnp.bfloat16)
        total = None
        for b in range(bands):
            filtered = None
            for table in reversed(tables[b]):
                term = jnp.dot(x, table, preferred_element_type=jnp.float32)
                filtered = term if filtered is None else filtered + term
            term = filtered * filtered * gain_ref[b]
            total = term if total is None else total + term
        parts.append(total.astype(jnp.bfloat16).astype(jnp.float32))
    mean = sum(jnp.sum(part, axis=1, keepdims=True) for part in parts) / WLEN
    vis = vis_ref[...]
    for j, part in enumerate(parts):
        out = ((part - mean) * vis).astype(jnp.bfloat16)
        win_ref[:, j * LANES : (j + 1) * LANES] = out.astype(jnp.float32)


def stack_kernel(n, delays_ref, win_ref, out_ref, hankel, total, sent, got, send_sem, recv_sem):
    sta = delays_ref.shape[0]
    block = out_ref.shape[1]
    me = lax.axis_index("sta")
    tile = lax.axis_index("tile")

    barrier = pltpu.get_barrier_semaphore()

    def greet(o, carry):
        pl.semaphore_signal(
            barrier, inc=1, device_id=(lax.rem(me + o, n), tile), device_id_type=MESH
        )
        return carry

    lax.fori_loop(1, n, greet, 0)

    def build(i, carry):
        for k in range(CHUNK):
            s = i * CHUNK + k
            rows = jnp.broadcast_to(win_ref[pl.ds(s, 1), :], (LANES, WLEN))
            rows = pltpu.roll(rows, WLEN - (LANES - 1), 1, stride=1, stride_axis=0)
            rows = rows[:, :L].astype(jnp.bfloat16)
            at = pl.ds(pl.multiple_of(s * D, D), D)
            for a in range(L // LANES):
                hankel[a * LANES : (a + 1) * LANES, at] = rows[:, a * LANES : (a + 1) * LANES]
        return carry

    lax.fori_loop(0, sta // CHUNK, build, 0)

    step = 16
    levels = [
        (lax.broadcasted_iota(jnp.int32, (step, block), 0) + k * step)
        .astype(jnp.float32)
        .astype(jnp.bfloat16)
        for k in range(D // step)
    ]
    one = jnp.ones((step, block), jnp.bfloat16)
    zero = jnp.zeros((step, block), jnp.bfloat16)

    def stack(owner):
        columns = pl.ds(pl.multiple_of(owner * block, block), block)
        total[...] = jnp.zeros_like(total)

        def add(c, carry):
            near = delays_ref[pl.ds(pl.multiple_of(c * CHUNK, CHUNK), CHUNK), columns].astype(
                jnp.float32
            )
            pieces = []
            for k in range(CHUNK):
                row = jnp.broadcast_to(near[k : k + 1, :], (step, block)).astype(jnp.bfloat16)
                pieces.extend(jnp.where(row == level, one, zero) for level in levels)
            onehot = jnp.concatenate(pieces, axis=0)
            depth = CHUNK * D
            lhs = hankel[:, pl.ds(pl.multiple_of(c * depth, depth), depth)]
            total[...] += jnp.dot(lhs, onehot, preferred_element_type=jnp.float32)
            return carry

        lax.fori_loop(0, sta // CHUNK, add, 0)

    def copy_of(o):
        return pltpu.make_async_remote_copy(
            src_ref=sent.at[o - 1],
            dst_ref=got.at[o - 1],
            send_sem=send_sem.at[o - 1],
            recv_sem=recv_sem.at[o - 1],
            device_id=(lax.rem(me + o, n), tile),
            device_id_type=MESH,
        )

    pl.semaphore_wait(barrier, n - 1)

    def send(o, carry):
        stack(lax.rem(me + o, n))
        sent[o - 1] = total[...].astype(jnp.bfloat16)
        copy_of(o).start()
        return carry

    lax.fori_loop(1, n, send, 0)
    stack(me)

    def collect(o, carry):
        copy_of(o).wait()
        total[...] += got[o - 1].astype(jnp.float32)
        return carry

    lax.fori_loop(1, n, collect, 0)
    out_ref[...] = total[...] * (1.0 / math.sqrt(sta * n))


def on_device(traces, fir_taps, band_gain, starts, delays, visibility):
    sta = traces.shape[0]
    n = lax.axis_size("sta")
    tile_pos = lax.axis_index("tile")
    gathered = lax.all_gather(traces, "tile", axis=1, tiled=True)
    begin_at = lax.dynamic_index_in_dim(starts, tile_pos, 1, keepdims=False)
    visible = lax.dynamic_index_in_dim(visibility, tile_pos, 1, keepdims=True).astype(jnp.float32)
    padded_taps = jnp.pad(fir_taps, ((0, 0), (2 * LANES - TAPS, 0)))
    samp = gathered.shape[1]
    vmem = pl.BlockSpec(memory_space=pltpu.VMEM)
    smem = pl.BlockSpec(memory_space=pltpu.SMEM)
    windows = pl.pallas_call(
        window_kernel,
        out_shape=jax.ShapeDtypeStruct((sta, WLEN), jnp.float32),
        in_specs=[smem, smem, vmem, vmem, vmem],
        out_specs=vmem,
        scratch_shapes=[
            pltpu.VMEM((sta, samp + 2 * LANES), jnp.float32),
            pltpu.VMEM((sta, 4 * LANES), jnp.float32),
        ],
        compiler_params=pltpu.CompilerParams(vmem_limit_bytes=40 * 2**20),
        name="windows",
    )(begin_at, band_gain, gathered, padded_taps, visible)
    grid = delays.shape[1]
    block = grid // n
    image = pl.pallas_call(
        functools.partial(stack_kernel, n),
        out_shape=jax.ShapeDtypeStruct((L, block), jnp.float32),
        in_specs=[vmem, vmem],
        out_specs=vmem,
        scratch_shapes=[
            pltpu.VMEM((L, sta * D), jnp.bfloat16),
            pltpu.VMEM((L, block), jnp.float32),
            pltpu.VMEM((n - 1, L, block), jnp.bfloat16),
            pltpu.VMEM((n - 1, L, block), jnp.bfloat16),
            pltpu.SemaphoreType.DMA((n - 1,)),
            pltpu.SemaphoreType.DMA((n - 1,)),
        ],
        compiler_params=pltpu.CompilerParams(
            collective_id=0, has_side_effects=True, vmem_limit_bytes=48 * 2**20
        ),
        name="stack",
    )(delays, windows)
    lagged = jnp.flip(image.reshape(L // LANES, LANES, block), 1).reshape(L, block)
    return lagged.T


def solution(mesh):
    placed = (P("sta", "tile"), P(), P(), P("sta", None), P("sta", "tile"), P("sta", None))
    return jax.shard_map(
        on_device, mesh=mesh, in_specs=placed, out_specs=P(("tile", "sta"), None), check_vma=False
    )
```

```python
import functools
import math

import jax
import jax.numpy as jnp
from jax import lax
from jax.experimental import pallas as pl
from jax.experimental.pallas import tpu as pltpu
from jax.sharding import PartitionSpec as P

TAPS = 64
D = 128
L = 256
WLEN = 384
LANES = 128
CHUNK = 32
MESH = pl.DeviceIdType.MESH


def window_kernel(starts_ref, gain_ref, traces_ref, taps_ref, vis_ref, win_ref, padded, held):
    sta, samp = traces_ref.shape
    bands = taps_ref.shape[0]
    padded[:, :LANES] = jnp.zeros((sta, LANES), jnp.float32)
    padded[:, LANES + samp :] = jnp.zeros((sta, LANES), jnp.float32)
    padded[:, LANES : LANES + samp] = traces_ref[...].astype(jnp.float32)

    def take(i, carry):
        for k in range(CHUNK):
            s = i * CHUNK + k
            first = starts_ref[s] + (LANES - TAPS)
            whole = first // LANES
            row = padded[pl.ds(s, 1), pl.ds(pl.multiple_of(whole * LANES, LANES), 5 * LANES)]
            row = pltpu.roll(row, 5 * LANES - (first - whole * LANES), 1)
            held[pl.ds(s, 1), :] = row[:, : 4 * LANES]
        return carry

    lax.fori_loop(0, sta // CHUNK, take, 0)

    tables = []
    for b in range(bands):
        rows = jnp.broadcast_to(taps_ref[b : b + 1, :], (2 * LANES, 2 * LANES))
        table = pltpu.roll(rows, 0, 1, stride=1, stride_axis=0)[:, :LANES]
        high = table.astype(jnp.bfloat16)
        rest = table - high.astype(jnp.float32)
        mid = rest.astype(jnp.bfloat16)
        low = (rest - mid.astype(jnp.float32)).astype(jnp.bfloat16)
        tables.append(jnp.concatenate([low, mid, high], axis=0))
    table = jnp.concatenate(tables, axis=1)
    parts = []
    for j in range(WLEN // LANES):
        x = held[:, j * LANES : (j + 2) * LANES].astype(jnp.bfloat16)
        x = jnp.concatenate([x, x, x], axis=1)
        filtered = jnp.dot(x, table, preferred_element_type=jnp.float32)
        total = None
        for b in range(bands):
            band = filtered[:, b * LANES : (b + 1) * LANES]
            term = band * band * gain_ref[b]
            total = term if total is None else total + term
        parts.append(total.astype(jnp.bfloat16).astype(jnp.float32))
    mean = sum(jnp.sum(part, axis=1, keepdims=True) for part in parts) / WLEN
    vis = vis_ref[...]
    for j, part in enumerate(parts):
        out = ((part - mean) * vis).astype(jnp.bfloat16)
        win_ref[:, j * LANES : (j + 1) * LANES] = out.astype(jnp.float32)


def stack_kernel(n, delays_ref, win_ref, out_ref, hankel, total, sent, got, send_sem, recv_sem):
    sta = delays_ref.shape[0]
    block = out_ref.shape[1]
    me = lax.axis_index("sta")
    tile = lax.axis_index("tile")

    barrier = pltpu.get_barrier_semaphore()

    def greet(o, carry):
        pl.semaphore_signal(
            barrier, inc=1, device_id=(lax.rem(me + o, n), tile), device_id_type=MESH
        )
        return carry

    lax.fori_loop(1, n, greet, 0)

    step = 16

    def build(i, carry):
        for k in range(CHUNK):
            s = i * CHUNK + k
            rows = jnp.broadcast_to(win_ref[pl.ds(s, 1), :], (step, WLEN))
            rows = pltpu.roll(rows, WLEN - (step - 1), 1, stride=1, stride_axis=0)
            rows = rows.astype(jnp.bfloat16)
            at = pl.ds(pl.multiple_of(s * D, D), D)
            for m in range(LANES // step):
                by = LANES - step - m * step
                moved = pltpu.roll(rows, WLEN - by, 1) if by else rows
                for a in range(L // LANES):
                    first = a * LANES + m * step
                    hankel[first : first + step, at] = moved[:, a * LANES : (a + 1) * LANES]
        return carry

    lax.fori_loop(0, sta // CHUNK, build, 0)

    levels = [
        (lax.broadcasted_iota(jnp.int32, (step, block), 0) + k * step)
        .astype(jnp.float32)
        .astype(jnp.bfloat16)
        for k in range(D // step)
    ]
    one = jnp.ones((step, block), jnp.bfloat16)
    zero = jnp.zeros((step, block), jnp.bfloat16)

    def stack(owner):
        columns = pl.ds(pl.multiple_of(owner * block, block), block)
        total[...] = jnp.zeros_like(total)

        def add(c, carry):
            near = delays_ref[pl.ds(pl.multiple_of(c * CHUNK, CHUNK), CHUNK), columns].astype(
                jnp.float32
            )
            sums = []
            depth = CHUNK // 2 * D
            for half in range(2):
                pieces = []
                for k in range(half * CHUNK // 2, (half + 1) * CHUNK // 2):
                    row = jnp.broadcast_to(near[k : k + 1, :], (step, block)).astype(jnp.bfloat16)
                    pieces.extend(jnp.where(row == level, one, zero) for level in levels)
                onehot = jnp.concatenate(pieces, axis=0)
                lhs = hankel[:, pl.ds(pl.multiple_of((2 * c + half) * depth, depth), depth)]
                sums.append(jnp.dot(lhs, onehot, preferred_element_type=jnp.float32))
            total[...] += sums[0] + sums[1]
            return carry

        lax.fori_loop(0, sta // CHUNK, add, 0)

    def copy_of(o):
        return pltpu.make_async_remote_copy(
            src_ref=sent.at[o - 1],
            dst_ref=got.at[o - 1],
            send_sem=send_sem.at[o - 1],
            recv_sem=recv_sem.at[o - 1],
            device_id=(lax.rem(me + o, n), tile),
            device_id_type=MESH,
        )

    pl.semaphore_wait(barrier, n - 1)

    def send(o, carry):
        stack(lax.rem(me + o, n))

        @pl.when(o < n)
        def _():
            sent[o - 1] = total[...].astype(jnp.bfloat16)
            copy_of(o).start()

        return carry

    lax.fori_loop(1, n + 1, send, 0)

    def collect(o, carry):
        copy_of(o).wait()
        total[...] += got[o - 1].astype(jnp.float32)
        return carry

    lax.fori_loop(1, n, collect, 0)
    out_ref[...] = total[...] * (1.0 / math.sqrt(sta * n))


def on_device(traces, fir_taps, band_gain, starts, delays, visibility):
    sta = traces.shape[0]
    n = lax.axis_size("sta")
    tile_pos = lax.axis_index("tile")
    gathered = lax.all_gather(traces, "tile", axis=1, tiled=True)
    begin_at = lax.dynamic_index_in_dim(starts, tile_pos, 1, keepdims=False)
    visible = lax.dynamic_index_in_dim(visibility, tile_pos, 1, keepdims=True).astype(jnp.float32)
    padded_taps = jnp.pad(fir_taps, ((0, 0), (2 * LANES - TAPS, 0)))
    samp = gathered.shape[1]
    vmem = pl.BlockSpec(memory_space=pltpu.VMEM)
    smem = pl.BlockSpec(memory_space=pltpu.SMEM)
    windows = pl.pallas_call(
        window_kernel,
        out_shape=jax.ShapeDtypeStruct((sta, WLEN), jnp.float32),
        in_specs=[smem, smem, vmem, vmem, vmem],
        out_specs=vmem,
        scratch_shapes=[
            pltpu.VMEM((sta, samp + 2 * LANES), jnp.float32),
            pltpu.VMEM((sta, 4 * LANES), jnp.float32),
        ],
        compiler_params=pltpu.CompilerParams(vmem_limit_bytes=40 * 2**20),
        name="windows",
    )(begin_at, band_gain, gathered, padded_taps, visible)
    grid = delays.shape[1]
    block = grid // n
    image = pl.pallas_call(
        functools.partial(stack_kernel, n),
        out_shape=jax.ShapeDtypeStruct((L, block), jnp.float32),
        in_specs=[vmem, vmem],
        out_specs=vmem,
        scratch_shapes=[
            pltpu.VMEM((L, sta * D), jnp.bfloat16),
            pltpu.VMEM((L, block), jnp.float32),
            pltpu.VMEM((n - 1, L, block), jnp.bfloat16),
            pltpu.VMEM((n - 1, L, block), jnp.bfloat16),
            pltpu.SemaphoreType.DMA((n - 1,)),
            pltpu.SemaphoreType.DMA((n - 1,)),
        ],
        compiler_params=pltpu.CompilerParams(
            collective_id=0, has_side_effects=True, vmem_limit_bytes=48 * 2**20
        ),
        name="stack",
    )(delays, windows)
    lagged = jnp.flip(image.reshape(L // LANES, LANES, block), 1).reshape(L, block)
    return lagged.T


def solution(mesh):
    placed = (P("sta", "tile"), P(), P(), P("sta", None), P("sta", "tile"), P("sta", None))
    return jax.shard_map(
        on_device, mesh=mesh, in_specs=placed, out_specs=P(("tile", "sta"), None), check_vma=False
    )
```

```python
import functools
import math

import jax
import jax.numpy as jnp
from jax import lax
from jax.experimental import pallas as pl
from jax.experimental.pallas import tpu as pltpu
from jax.sharding import PartitionSpec as P

TAPS = 64
D = 128
L = 256
WLEN = 384
LANES = 128
CHUNK = 32
MESH = pl.DeviceIdType.MESH


def window_kernel(starts_ref, gain_ref, traces_ref, taps_ref, vis_ref, win_ref, padded, held):
    sta, samp = traces_ref.shape
    bands = taps_ref.shape[0]
    padded[:, :LANES] = jnp.zeros((sta, LANES), jnp.float32)
    padded[:, LANES + samp :] = jnp.zeros((sta, LANES), jnp.float32)
    padded[:, LANES : LANES + samp] = traces_ref[...].astype(jnp.float32)

    def take(i, carry):
        for k in range(CHUNK):
            s = i * CHUNK + k
            first = starts_ref[s] + (LANES - TAPS)
            whole = first // LANES
            row = padded[pl.ds(s, 1), pl.ds(pl.multiple_of(whole * LANES, LANES), 5 * LANES)]
            row = pltpu.roll(row, 5 * LANES - (first - whole * LANES), 1)
            held[pl.ds(s, 1), :] = row[:, : 4 * LANES]
        return carry

    lax.fori_loop(0, sta // CHUNK, take, 0)

    tables = []
    for b in range(bands):
        rows = jnp.broadcast_to(taps_ref[b : b + 1, :], (2 * LANES, 2 * LANES))
        table = pltpu.roll(rows, 0, 1, stride=1, stride_axis=0)[:, :LANES]
        high = table.astype(jnp.bfloat16)
        rest = table - high.astype(jnp.float32)
        mid = rest.astype(jnp.bfloat16)
        low = (rest - mid.astype(jnp.float32)).astype(jnp.bfloat16)
        tables.append(jnp.concatenate([low, mid, high], axis=0))
    table = jnp.concatenate(tables, axis=1)
    parts = []
    for j in range(WLEN // LANES):
        x = held[:, j * LANES : (j + 2) * LANES].astype(jnp.bfloat16)
        x = jnp.concatenate([x, x, x], axis=1)
        filtered = jnp.dot(x, table, preferred_element_type=jnp.float32)
        total = None
        for b in range(bands):
            band = filtered[:, b * LANES : (b + 1) * LANES]
            term = band * band * gain_ref[b]
            total = term if total is None else total + term
        parts.append(total.astype(jnp.bfloat16).astype(jnp.float32))
    mean = sum(jnp.sum(part, axis=1, keepdims=True) for part in parts) / WLEN
    vis = vis_ref[...]
    for j, part in enumerate(parts):
        out = ((part - mean) * vis).astype(jnp.bfloat16)
        win_ref[:, j * LANES : (j + 1) * LANES] = out.astype(jnp.float32)


def stack_kernel(n, delays_ref, win_ref, out_ref, hankel, total, sent, got, send_sem, recv_sem):
    sta = delays_ref.shape[0]
    block = out_ref.shape[1]
    me = lax.axis_index("sta")
    tile = lax.axis_index("tile")

    barrier = pltpu.get_barrier_semaphore()

    def greet(o, carry):
        pl.semaphore_signal(
            barrier, inc=1, device_id=(lax.rem(me + o, n), tile), device_id_type=MESH
        )
        return carry

    lax.fori_loop(1, n, greet, 0)

    step = 16

    def build(i, carry):
        for k in range(CHUNK):
            s = i * CHUNK + k
            rows = jnp.broadcast_to(win_ref[pl.ds(s, 1), :], (step, WLEN))
            rows = pltpu.roll(rows, WLEN - (step - 1), 1, stride=1, stride_axis=0)
            rows = rows.astype(jnp.bfloat16)
            at = pl.ds(pl.multiple_of(s * D, D), D)
            for m in range(LANES // step):
                by = LANES - step - m * step
                moved = pltpu.roll(rows, WLEN - by, 1) if by else rows
                for a in range(L // LANES):
                    first = a * LANES + m * step
                    hankel[first : first + step, at] = moved[:, a * LANES : (a + 1) * LANES]
        return carry

    lax.fori_loop(0, sta // CHUNK, build, 0)

    levels = [
        (lax.broadcasted_iota(jnp.int32, (step, 2 * block), 0) + k * step)
        .astype(jnp.float32)
        .astype(jnp.bfloat16)
        for k in range(D // step)
    ]
    one = jnp.ones((step, 2 * block), jnp.bfloat16)
    zero = jnp.zeros((step, 2 * block), jnp.bfloat16)

    def columns_of(o):
        return pl.ds(pl.multiple_of(lax.rem(me + o, n) * block, block), block)

    def stack(first, last):
        total[...] = jnp.zeros_like(total)

        def add(c, carry):
            rows = pl.ds(pl.multiple_of(c * CHUNK, CHUNK), CHUNK)
            near = jnp.concatenate(
                [delays_ref[rows, columns_of(first)], delays_ref[rows, columns_of(last)]], axis=1
            ).astype(jnp.float32)
            pieces = []
            for k in range(CHUNK):
                row = jnp.broadcast_to(near[k : k + 1, :], (step, 2 * block)).astype(jnp.bfloat16)
                pieces.extend(jnp.where(row == level, one, zero) for level in levels)
            onehot = jnp.concatenate(pieces, axis=0)
            depth = CHUNK * D
            lhs = hankel[:, pl.ds(pl.multiple_of(c * depth, depth), depth)]
            total[...] += jnp.dot(lhs, onehot, preferred_element_type=jnp.float32)
            return carry

        lax.fori_loop(0, sta // CHUNK, add, 0)

    def copy_of(o):
        return pltpu.make_async_remote_copy(
            src_ref=sent.at[o - 1],
            dst_ref=got.at[o - 1],
            send_sem=send_sem.at[o - 1],
            recv_sem=recv_sem.at[o - 1],
            device_id=(lax.rem(me + o, n), tile),
            device_id_type=MESH,
        )

    pl.semaphore_wait(barrier, n - 1)

    def send(pair, carry):
        o = 2 * pair + 1
        stack(o, o + 1)
        sent[o - 1] = total[:, :block].astype(jnp.bfloat16)
        copy_of(o).start()

        @pl.when(o + 1 < n)
        def _():
            sent[o] = total[:, block:].astype(jnp.bfloat16)
            copy_of(o + 1).start()

        return carry

    lax.fori_loop(0, n // 2, send, 0)
    image = total[:, block:]
    for o in range(1, n):
        copy_of(o).wait()
        image += got[o - 1].astype(jnp.float32)
    out_ref[...] = image * (1.0 / math.sqrt(sta * n))


def on_device(traces, fir_taps, band_gain, starts, delays, visibility):
    sta = traces.shape[0]
    n = lax.axis_size("sta")
    tile_pos = lax.axis_index("tile")
    gathered = lax.all_gather(traces, "tile", axis=1, tiled=True)
    begin_at = lax.dynamic_index_in_dim(starts, tile_pos, 1, keepdims=False)
    visible = lax.dynamic_index_in_dim(visibility, tile_pos, 1, keepdims=True).astype(jnp.float32)
    padded_taps = jnp.pad(fir_taps, ((0, 0), (2 * LANES - TAPS, 0)))
    samp = gathered.shape[1]
    vmem = pl.BlockSpec(memory_space=pltpu.VMEM)
    smem = pl.BlockSpec(memory_space=pltpu.SMEM)
    windows = pl.pallas_call(
        window_kernel,
        out_shape=jax.ShapeDtypeStruct((sta, WLEN), jnp.float32),
        in_specs=[smem, smem, vmem, vmem, vmem],
        out_specs=vmem,
        scratch_shapes=[
            pltpu.VMEM((sta, samp + 2 * LANES), jnp.float32),
            pltpu.VMEM((sta, 4 * LANES), jnp.float32),
        ],
        compiler_params=pltpu.CompilerParams(vmem_limit_bytes=40 * 2**20),
        name="windows",
    )(begin_at, band_gain, gathered, padded_taps, visible)
    grid = delays.shape[1]
    block = grid // n
    image = pl.pallas_call(
        functools.partial(stack_kernel, n),
        out_shape=jax.ShapeDtypeStruct((L, block), jnp.float32),
        in_specs=[vmem, vmem],
        out_specs=vmem,
        scratch_shapes=[
            pltpu.VMEM((L, sta * D), jnp.bfloat16),
            pltpu.VMEM((L, 2 * block), jnp.float32),
            pltpu.VMEM((n - 1, L, block), jnp.bfloat16),
            pltpu.VMEM((n - 1, L, block), jnp.bfloat16),
            pltpu.SemaphoreType.DMA((n - 1,)),
            pltpu.SemaphoreType.DMA((n - 1,)),
        ],
        compiler_params=pltpu.CompilerParams(
            collective_id=0, has_side_effects=True, vmem_limit_bytes=48 * 2**20
        ),
        name="stack",
    )(delays, windows)
    lagged = jnp.flip(image.reshape(L // LANES, LANES, block), 1).reshape(L, block)
    return lagged.T


def solution(mesh):
    placed = (P("sta", "tile"), P(), P(), P("sta", None), P("sta", "tile"), P("sta", None))
    return jax.shard_map(
        on_device, mesh=mesh, in_specs=placed, out_specs=P(("tile", "sta"), None), check_vma=False
    )
```

```python
import functools
import math

import jax
import jax.numpy as jnp
from jax import lax
from jax.experimental import pallas as pl
from jax.experimental.pallas import tpu as pltpu
from jax.sharding import PartitionSpec as P

TAPS = 64
D = 128
L = 256
WLEN = 384
LANES = 128
CHUNK = 32
EIGHT = jnp.float8_e4m3fn
MESH = pl.DeviceIdType.MESH


def window_kernel(starts_ref, gain_ref, traces_ref, taps_ref, vis_ref, win_ref, unit_ref, padded, held):
    sta, samp = traces_ref.shape
    bands = taps_ref.shape[0]
    padded[:, :LANES] = jnp.zeros((sta, LANES), jnp.float32)
    padded[:, LANES + samp :] = jnp.zeros((sta, LANES), jnp.float32)
    padded[:, LANES : LANES + samp] = traces_ref[...].astype(jnp.float32)

    def take(i, carry):
        for k in range(CHUNK):
            s = i * CHUNK + k
            first = starts_ref[s] + (LANES - TAPS)
            whole = first // LANES
            row = padded[pl.ds(s, 1), pl.ds(pl.multiple_of(whole * LANES, LANES), 5 * LANES)]
            row = pltpu.roll(row, 5 * LANES - (first - whole * LANES), 1)
            held[pl.ds(s, 1), :] = row[:, : 4 * LANES]
        return carry

    lax.fori_loop(0, sta // CHUNK, take, 0)

    tables = []
    for b in range(bands):
        rows = jnp.broadcast_to(taps_ref[b : b + 1, :], (2 * LANES, 2 * LANES))
        table = pltpu.roll(rows, 0, 1, stride=1, stride_axis=0)[:, :LANES]
        high = table.astype(jnp.bfloat16)
        rest = table - high.astype(jnp.float32)
        mid = rest.astype(jnp.bfloat16)
        low = (rest - mid.astype(jnp.float32)).astype(jnp.bfloat16)
        tables.append(jnp.concatenate([low, mid, high], axis=0))
    table = jnp.concatenate(tables, axis=1)
    parts = []
    for j in range(WLEN // LANES):
        x = held[:, j * LANES : (j + 2) * LANES].astype(jnp.bfloat16)
        x = jnp.concatenate([x, x, x], axis=1)
        filtered = jnp.dot(x, table, preferred_element_type=jnp.float32)
        total = None
        for b in range(bands):
            band = filtered[:, b * LANES : (b + 1) * LANES]
            term = band * band * gain_ref[b]
            total = term if total is None else total + term
        parts.append(total.astype(jnp.bfloat16).astype(jnp.float32))
    mean = sum(jnp.sum(part, axis=1, keepdims=True) for part in parts) / WLEN
    vis = vis_ref[...]
    parts = [((part - mean) * vis).astype(jnp.bfloat16).astype(jnp.float32) for part in parts]
    largest = functools.reduce(jnp.maximum, [jnp.max(jnp.abs(part), keepdims=True) for part in parts])
    largest = largest * 2.0**-14
    scale = jnp.full((1, 1), 2.0**-14, jnp.float32)
    unit = jnp.full((1, 1), 2.0**14, jnp.float32)
    for p in (64, 32, 16, 8, 4, 2, 1):
        small = largest * 2.0**p < 256.0
        largest = jnp.where(small, largest * 2.0**p, largest)
        scale = jnp.where(small, scale * 2.0**p, scale)
        unit = jnp.where(small, unit * 2.0**-p, unit)
    unit_ref[...] = unit
    for j, part in enumerate(parts):
        scaled = part * scale
        high = scaled.astype(EIGHT).astype(jnp.float32)
        at = slice(j * LANES, (j + 1) * LANES)
        win_ref[0, :, at] = high
        win_ref[1, :, at] = (scaled - high) * 16.0


def stack_kernel(n, delays_ref, win_ref, unit_ref, out_ref, hankel, total, sent, got, send_sem, recv_sem):
    sta = delays_ref.shape[0]
    block = out_ref.shape[1]
    me = lax.axis_index("sta")
    tile = lax.axis_index("tile")

    barrier = pltpu.get_barrier_semaphore()

    def greet(o, carry):
        pl.semaphore_signal(
            barrier, inc=1, device_id=(lax.rem(me + o, n), tile), device_id_type=MESH
        )
        return carry

    lax.fori_loop(1, n, greet, 0)

    step = 32

    def build(i, carry):
        for k in range(CHUNK // 2):
            s = i * (CHUNK // 2) + k
            at = pl.ds(pl.multiple_of(s * D, D), D)
            for term in range(2):
                rows = jnp.broadcast_to(win_ref[term, pl.ds(s, 1), :], (step, WLEN))
                rows = pltpu.roll(rows, WLEN - (step - 1), 1, stride=1, stride_axis=0)
                rows = rows.astype(EIGHT)
                for m in range(LANES // step):
                    by = LANES - step - m * step
                    moved = pltpu.roll(rows, WLEN - by, 1) if by else rows
                    moved = moved[:, :L].astype(EIGHT)
                    for a in range(L // LANES):
                        first = term * L + a * LANES + m * step
                        hankel[first : first + step, at] = moved[:, a * LANES : (a + 1) * LANES]
        return carry

    lax.fori_loop(0, sta // (CHUNK // 2), build, 0)

    levels = [
        (lax.broadcasted_iota(jnp.int32, (step, block), 0) + k * step)
        .astype(jnp.float32)
        .astype(jnp.bfloat16)
        for k in range(D // step)
    ]
    one = jnp.ones((step, block), jnp.bfloat16)
    zero = jnp.zeros((step, block), jnp.bfloat16)

    unit = unit_ref[...]

    def stack(owner):
        columns = pl.ds(pl.multiple_of(owner * block, block), block)
        total[...] = jnp.zeros_like(total)

        def add(c, carry):
            near = delays_ref[pl.ds(pl.multiple_of(c * CHUNK, CHUNK), CHUNK), columns].astype(
                jnp.float32
            )
            sums = []
            depth = CHUNK // 2 * D
            for half in range(2):
                pieces = []
                for k in range(half * CHUNK // 2, (half + 1) * CHUNK // 2):
                    row = jnp.broadcast_to(near[k : k + 1, :], (step, block)).astype(jnp.bfloat16)
                    pieces.extend(
                        jnp.where(row == level, one, zero).astype(EIGHT) for level in levels
                    )
                onehot = jnp.concatenate(pieces, axis=0)
                lhs = hankel[:, pl.ds(pl.multiple_of((2 * c + half) * depth, depth), depth)]
                sums.append(jnp.dot(lhs, onehot, preferred_element_type=jnp.float32))
            both = sums[0] + sums[1]
            total[...] += both[:L] + both[L:] * (1.0 / 16.0)
            return carry

        lax.fori_loop(0, sta // CHUNK, add, 0)

    def copy_of(o):
        return pltpu.make_async_remote_copy(
            src_ref=sent.at[o - 1],
            dst_ref=got.at[o - 1],
            send_sem=send_sem.at[o - 1],
            recv_sem=recv_sem.at[o - 1],
            device_id=(lax.rem(me + o, n), tile),
            device_id_type=MESH,
        )

    pl.semaphore_wait(barrier, n - 1)

    def send(o, carry):
        stack(lax.rem(me + o, n))

        @pl.when(o < n)
        def _():
            sent[o - 1] = (total[...] * unit).astype(jnp.bfloat16)
            copy_of(o).start()

        return carry

    lax.fori_loop(1, n + 1, send, 0)
    total[...] *= unit

    def collect(o, carry):
        copy_of(o).wait()
        total[...] += got[o - 1].astype(jnp.float32)
        return carry

    lax.fori_loop(1, n, collect, 0)
    out_ref[...] = total[...] * (1.0 / math.sqrt(sta * n))


def on_device(traces, fir_taps, band_gain, starts, delays, visibility):
    sta = traces.shape[0]
    n = lax.axis_size("sta")
    tile_pos = lax.axis_index("tile")
    gathered = lax.all_gather(traces, "tile", axis=1, tiled=True)
    begin_at = lax.dynamic_index_in_dim(starts, tile_pos, 1, keepdims=False)
    visible = lax.dynamic_index_in_dim(visibility, tile_pos, 1, keepdims=True).astype(jnp.float32)
    padded_taps = jnp.pad(fir_taps, ((0, 0), (2 * LANES - TAPS, 0)))
    samp = gathered.shape[1]
    vmem = pl.BlockSpec(memory_space=pltpu.VMEM)
    smem = pl.BlockSpec(memory_space=pltpu.SMEM)
    windows, unit = pl.pallas_call(
        window_kernel,
        out_shape=[
            jax.ShapeDtypeStruct((2, sta, WLEN), jnp.float32),
            jax.ShapeDtypeStruct((1, 1), jnp.float32),
        ],
        in_specs=[smem, smem, vmem, vmem, vmem],
        out_specs=[vmem, vmem],
        scratch_shapes=[
            pltpu.VMEM((sta, samp + 2 * LANES), jnp.float32),
            pltpu.VMEM((sta, 4 * LANES), jnp.float32),
        ],
        compiler_params=pltpu.CompilerParams(vmem_limit_bytes=40 * 2**20),
        name="windows",
    )(begin_at, band_gain, gathered, padded_taps, visible)
    grid = delays.shape[1]
    block = grid // n
    image = pl.pallas_call(
        functools.partial(stack_kernel, n),
        out_shape=jax.ShapeDtypeStruct((L, block), jnp.float32),
        in_specs=[vmem, vmem, vmem],
        out_specs=vmem,
        scratch_shapes=[
            pltpu.VMEM((2 * L, sta * D), EIGHT),
            pltpu.VMEM((L, block), jnp.float32),
            pltpu.VMEM((n - 1, L, block), jnp.bfloat16),
            pltpu.VMEM((n - 1, L, block), jnp.bfloat16),
            pltpu.SemaphoreType.DMA((n - 1,)),
            pltpu.SemaphoreType.DMA((n - 1,)),
        ],
        compiler_params=pltpu.CompilerParams(
            collective_id=0, has_side_effects=True, vmem_limit_bytes=48 * 2**20
        ),
        name="stack",
    )(delays, windows, unit)
    lagged = jnp.flip(image.reshape(L // LANES, LANES, block), 1).reshape(L, block)
    return lagged.T


def solution(mesh):
    placed = (P("sta", "tile"), P(), P(), P("sta", None), P("sta", "tile"), P("sta", None))
    return jax.shard_map(
        on_device, mesh=mesh, in_specs=placed, out_specs=P(("tile", "sta"), None), check_vma=False
    )
```

```python
import functools
import math

import jax
import jax.numpy as jnp
from jax import lax
from jax.experimental import pallas as pl
from jax.experimental.pallas import tpu as pltpu
from jax.sharding import PartitionSpec as P

TAPS = 64
D = 128
L = 256
WLEN = 384
LANES = 128
CHUNK = 32
MESH = pl.DeviceIdType.MESH


def window_kernel(starts_ref, gain_ref, traces_ref, taps_ref, vis_ref, win_ref, padded, held):
    sta, samp = traces_ref.shape
    bands = taps_ref.shape[0]
    padded[:, :LANES] = jnp.zeros((sta, LANES), jnp.float32)
    padded[:, LANES + samp :] = jnp.zeros((sta, LANES), jnp.float32)
    padded[:, LANES : LANES + samp] = traces_ref[...].astype(jnp.float32)

    def take(i, carry):
        for k in range(CHUNK):
            s = i * CHUNK + k
            first = starts_ref[s] + (LANES - TAPS)
            whole = first // LANES
            row = padded[pl.ds(s, 1), pl.ds(pl.multiple_of(whole * LANES, LANES), 5 * LANES)]
            row = pltpu.roll(row, 5 * LANES - (first - whole * LANES), 1)
            held[pl.ds(s, 1), :] = row[:, : 4 * LANES]
        return carry

    lax.fori_loop(0, sta // CHUNK, take, 0)

    tables = []
    for b in range(bands):
        rows = jnp.broadcast_to(taps_ref[b : b + 1, :], (2 * LANES, 2 * LANES))
        table = pltpu.roll(rows, 0, 1, stride=1, stride_axis=0)[:, :LANES]
        high = table.astype(jnp.bfloat16)
        rest = table - high.astype(jnp.float32)
        mid = rest.astype(jnp.bfloat16)
        low = (rest - mid.astype(jnp.float32)).astype(jnp.bfloat16)
        tables.append(jnp.concatenate([low, mid, high], axis=0))
    table = jnp.concatenate(tables, axis=1)
    parts = []
    for j in range(WLEN // LANES):
        x = held[:, j * LANES : (j + 2) * LANES].astype(jnp.bfloat16)
        x = jnp.concatenate([x, x, x], axis=1)
        filtered = jnp.dot(x, table, preferred_element_type=jnp.float32)
        total = None
        for b in range(bands):
            band = filtered[:, b * LANES : (b + 1) * LANES]
            term = band * band * gain_ref[b]
            total = term if total is None else total + term
        parts.append(total.astype(jnp.bfloat16).astype(jnp.float32))
    mean = sum(jnp.sum(part, axis=1, keepdims=True) for part in parts) / WLEN
    vis = vis_ref[...]
    for j, part in enumerate(parts):
        out = ((part - mean) * vis).astype(jnp.bfloat16)
        win_ref[:, j * LANES : (j + 1) * LANES] = out.astype(jnp.float32)


def stack_kernel(n, delays_ref, win_ref, out_ref, hankel, total, sent, got, send_sem, recv_sem):
    sta = delays_ref.shape[0]
    block = out_ref.shape[1]
    me = lax.axis_index("sta")
    tile = lax.axis_index("tile")

    barrier = pltpu.get_barrier_semaphore()

    def greet(o, carry):
        pl.semaphore_signal(
            barrier, inc=1, device_id=(lax.rem(me + o, n), tile), device_id_type=MESH
        )
        return carry

    lax.fori_loop(1, n, greet, 0)

    step = 16

    def build(i, carry):
        for k in range(CHUNK):
            s = i * CHUNK + k
            rows = jnp.broadcast_to(win_ref[pl.ds(s, 1), :], (step, WLEN))
            rows = pltpu.roll(rows, WLEN - (step - 1), 1, stride=1, stride_axis=0)
            rows = rows.astype(jnp.bfloat16)
            at = pl.ds(pl.multiple_of(s * D, D), D)
            for m in range(LANES // step):
                by = LANES - step - m * step
                moved = pltpu.roll(rows, WLEN - by, 1) if by else rows
                for a in range(L // LANES):
                    first = a * LANES + m * step
                    hankel[first : first + step, at] = moved[:, a * LANES : (a + 1) * LANES]
        return carry

    lax.fori_loop(0, sta // CHUNK, build, 0)

    level = lax.broadcasted_iota(jnp.int32, (D, block), 0)

    def stack(owner):
        columns = pl.ds(pl.multiple_of(owner * block, block), block)
        total[...] = jnp.zeros_like(total)

        def add(c, carry):
            near = delays_ref[pl.ds(pl.multiple_of(c * CHUNK, CHUNK), CHUNK), columns]
            sums = []
            depth = CHUNK // 2 * D
            for half in range(2):
                pieces = []
                for k in range(half * CHUNK // 2, (half + 1) * CHUNK // 2):
                    row = jnp.broadcast_to(near[k : k + 1, :], (D, block))
                    pieces.append(jnp.where(row == level, 1.0, 0.0).astype(jnp.bfloat16))
                onehot = jnp.concatenate(pieces, axis=0)
                lhs = hankel[:, pl.ds(pl.multiple_of((2 * c + half) * depth, depth), depth)]
                sums.append(jnp.dot(lhs, onehot, preferred_element_type=jnp.float32))
            total[...] += sums[0] + sums[1]
            return carry

        lax.fori_loop(0, sta // CHUNK, add, 0)

    def copy_of(o):
        return pltpu.make_async_remote_copy(
            src_ref=sent.at[o - 1],
            dst_ref=got.at[o - 1],
            send_sem=send_sem.at[o - 1],
            recv_sem=recv_sem.at[o - 1],
            device_id=(lax.rem(me + o, n), tile),
            device_id_type=MESH,
        )

    pl.semaphore_wait(barrier, n - 1)

    def send(o, carry):
        stack(lax.rem(me + o, n))

        @pl.when(o < n)
        def _():
            sent[o - 1] = total[...].astype(jnp.bfloat16)
            copy_of(o).start()

        return carry

    lax.fori_loop(1, n + 1, send, 0)

    def collect(o, carry):
        copy_of(o).wait()
        total[...] += got[o - 1].astype(jnp.float32)
        return carry

    lax.fori_loop(1, n, collect, 0)
    out_ref[...] = total[...] * (1.0 / math.sqrt(sta * n))


def on_device(traces, fir_taps, band_gain, starts, delays, visibility):
    sta = traces.shape[0]
    n = lax.axis_size("sta")
    tile_pos = lax.axis_index("tile")
    gathered = lax.all_gather(traces, "tile", axis=1, tiled=True)
    begin_at = lax.dynamic_index_in_dim(starts, tile_pos, 1, keepdims=False)
    visible = lax.dynamic_index_in_dim(visibility, tile_pos, 1, keepdims=True).astype(jnp.float32)
    padded_taps = jnp.pad(fir_taps, ((0, 0), (2 * LANES - TAPS, 0)))
    samp = gathered.shape[1]
    vmem = pl.BlockSpec(memory_space=pltpu.VMEM)
    smem = pl.BlockSpec(memory_space=pltpu.SMEM)
    windows = pl.pallas_call(
        window_kernel,
        out_shape=jax.ShapeDtypeStruct((sta, WLEN), jnp.float32),
        in_specs=[smem, smem, vmem, vmem, vmem],
        out_specs=vmem,
        scratch_shapes=[
            pltpu.VMEM((sta, samp + 2 * LANES), jnp.float32),
            pltpu.VMEM((sta, 4 * LANES), jnp.float32),
        ],
        compiler_params=pltpu.CompilerParams(vmem_limit_bytes=40 * 2**20),
        name="windows",
    )(begin_at, band_gain, gathered, padded_taps, visible)
    grid = delays.shape[1]
    block = grid // n
    image = pl.pallas_call(
        functools.partial(stack_kernel, n),
        out_shape=jax.ShapeDtypeStruct((L, block), jnp.float32),
        in_specs=[vmem, vmem],
        out_specs=vmem,
        scratch_shapes=[
            pltpu.VMEM((L, sta * D), jnp.bfloat16),
            pltpu.VMEM((L, block), jnp.float32),
            pltpu.VMEM((n - 1, L, block), jnp.bfloat16),
            pltpu.VMEM((n - 1, L, block), jnp.bfloat16),
            pltpu.SemaphoreType.DMA((n - 1,)),
            pltpu.SemaphoreType.DMA((n - 1,)),
        ],
        compiler_params=pltpu.CompilerParams(
            collective_id=0, has_side_effects=True, vmem_limit_bytes=48 * 2**20
        ),
        name="stack",
    )(delays, windows)
    lagged = jnp.flip(image.reshape(L // LANES, LANES, block), 1).reshape(L, block)
    return lagged.T


def solution(mesh):
    placed = (P("sta", "tile"), P(), P(), P("sta", None), P("sta", "tile"), P("sta", None))
    return jax.shard_map(
        on_device, mesh=mesh, in_specs=placed, out_specs=P(("tile", "sta"), None), check_vma=False
    )
```

```python
import functools
import math

import jax
import jax.numpy as jnp
from jax import lax
from jax.experimental import pallas as pl
from jax.experimental.pallas import tpu as pltpu
from jax.sharding import PartitionSpec as P

TAPS = 64
D = 128
L = 256
WLEN = 384
LANES = 128
CHUNK = 16
MESH = pl.DeviceIdType.MESH


def window_kernel(starts_ref, gain_ref, traces_ref, taps_ref, vis_ref, win_ref, padded, held):
    sta, samp = traces_ref.shape
    bands = taps_ref.shape[0]
    padded[:, :LANES] = jnp.zeros((sta, LANES), jnp.float32)
    padded[:, LANES + samp :] = jnp.zeros((sta, LANES), jnp.float32)
    padded[:, LANES : LANES + samp] = traces_ref[...].astype(jnp.float32)

    def take(i, carry):
        for k in range(CHUNK):
            s = i * CHUNK + k
            first = starts_ref[s] + (LANES - TAPS)
            whole = first // LANES
            row = padded[pl.ds(s, 1), pl.ds(pl.multiple_of(whole * LANES, LANES), 5 * LANES)]
            row = pltpu.roll(row, 5 * LANES - (first - whole * LANES), 1)
            held[pl.ds(s, 1), :] = row[:, : 4 * LANES]
        return carry

    lax.fori_loop(0, sta // CHUNK, take, 0)

    tables = []
    for b in range(bands):
        rows = jnp.broadcast_to(taps_ref[b : b + 1, :], (2 * LANES, 2 * LANES))
        table = pltpu.roll(rows, 0, 1, stride=1, stride_axis=0)[:, :LANES]
        high = table.astype(jnp.bfloat16)
        rest = table - high.astype(jnp.float32)
        mid = rest.astype(jnp.bfloat16)
        low = (rest - mid.astype(jnp.float32)).astype(jnp.bfloat16)
        tables.append(jnp.concatenate([low, mid, high], axis=0))
    table = jnp.concatenate(tables, axis=1)
    parts = []
    for j in range(WLEN // LANES):
        x = held[:, j * LANES : (j + 2) * LANES].astype(jnp.bfloat16)
        x = jnp.concatenate([x, x, x], axis=1)
        filtered = jnp.dot(x, table, preferred_element_type=jnp.float32)
        total = None
        for b in range(bands):
            band = filtered[:, b * LANES : (b + 1) * LANES]
            term = band * band * gain_ref[b]
            total = term if total is None else total + term
        parts.append(total.astype(jnp.bfloat16).astype(jnp.float32))
    mean = sum(jnp.sum(part, axis=1, keepdims=True) for part in parts) / WLEN
    vis = vis_ref[...]
    for j, part in enumerate(parts):
        out = ((part - mean) * vis).astype(jnp.bfloat16)
        win_ref[:, j * LANES : (j + 1) * LANES] = out.astype(jnp.float32)


def stack_kernel(n, delays_ref, win_ref, out_ref, hankel, total, sent, got, send_sem, recv_sem):
    sta = delays_ref.shape[0]
    block = out_ref.shape[0]
    me = lax.axis_index("sta")
    tile = lax.axis_index("tile")

    barrier = pltpu.get_barrier_semaphore()

    def greet(o, carry):
        pl.semaphore_signal(
            barrier, inc=1, device_id=(lax.rem(me + o, n), tile), device_id_type=MESH
        )
        return carry

    lax.fori_loop(1, n, greet, 0)

    step = 16

    def build(i, carry):
        for k in range(CHUNK):
            s = i * CHUNK + k
            rows = jnp.broadcast_to(win_ref[pl.ds(s, 1), :], (step, WLEN))
            rows = pltpu.roll(rows, WLEN - (step - 1), 1, stride=1, stride_axis=0)
            rows = rows.astype(jnp.bfloat16)
            for m in range(LANES // step):
                by = LANES - step - m * step
                moved = pltpu.roll(rows, WLEN - by, 1) if by else rows
                at = pl.ds(pl.multiple_of(s * D + m * step, step), step)
                hankel[at, :] = moved[:, :L]
        return carry

    lax.fori_loop(0, sta // CHUNK, build, 0)

    level = D - 1 - lax.broadcasted_iota(jnp.int32, (2 * block, D), 1)

    def columns_of(o):
        return pl.ds(pl.multiple_of(lax.rem(me + o, n) * block, block), block)

    def stack(first, last):
        total[...] = jnp.zeros_like(total)

        def add(c, carry):
            rows = pl.ds(pl.multiple_of(c * CHUNK, CHUNK), CHUNK)
            near = jnp.concatenate(
                [delays_ref[rows, columns_of(first)].T, delays_ref[rows, columns_of(last)].T],
                axis=0,
            )
            pieces = []
            for k in range(CHUNK):
                column = jnp.broadcast_to(near[:, k : k + 1], (2 * block, D))
                pieces.append(jnp.where(column == level, 1.0, 0.0).astype(jnp.bfloat16))
            onehot = jnp.concatenate(pieces, axis=1)
            depth = CHUNK * D
            rhs = hankel[pl.ds(pl.multiple_of(c * depth, depth), depth), :]
            total[...] += jnp.dot(onehot, rhs, preferred_element_type=jnp.float32)
            return carry

        lax.fori_loop(0, sta // CHUNK, add, 0)

    def copy_of(o):
        return pltpu.make_async_remote_copy(
            src_ref=sent.at[o - 1],
            dst_ref=got.at[o - 1],
            send_sem=send_sem.at[o - 1],
            recv_sem=recv_sem.at[o - 1],
            device_id=(lax.rem(me + o, n), tile),
            device_id_type=MESH,
        )

    pl.semaphore_wait(barrier, n - 1)

    def send(pair, carry):
        o = 2 * pair + 1
        stack(o, o + 1)
        sent[o - 1] = total[:block, :].astype(jnp.bfloat16)
        copy_of(o).start()

        @pl.when(o + 1 < n)
        def _():
            sent[o] = total[block:, :].astype(jnp.bfloat16)
            copy_of(o + 1).start()

        return carry

    lax.fori_loop(0, n // 2, send, 0)
    image = total[block:, :]
    for o in range(1, n):
        copy_of(o).wait()
        image += got[o - 1].astype(jnp.float32)
    out_ref[...] = image * (1.0 / math.sqrt(sta * n))


def on_device(traces, fir_taps, band_gain, starts, delays, visibility):
    sta = traces.shape[0]
    n = lax.axis_size("sta")
    tile_pos = lax.axis_index("tile")
    gathered = lax.all_gather(traces, "tile", axis=1, tiled=True)
    begin_at = lax.dynamic_index_in_dim(starts, tile_pos, 1, keepdims=False)
    visible = lax.dynamic_index_in_dim(visibility, tile_pos, 1, keepdims=True).astype(jnp.float32)
    padded_taps = jnp.pad(fir_taps, ((0, 0), (2 * LANES - TAPS, 0)))
    samp = gathered.shape[1]
    vmem = pl.BlockSpec(memory_space=pltpu.VMEM)
    smem = pl.BlockSpec(memory_space=pltpu.SMEM)
    windows = pl.pallas_call(
        window_kernel,
        out_shape=jax.ShapeDtypeStruct((sta, WLEN), jnp.float32),
        in_specs=[smem, smem, vmem, vmem, vmem],
        out_specs=vmem,
        scratch_shapes=[
            pltpu.VMEM((sta, samp + 2 * LANES), jnp.float32),
            pltpu.VMEM((sta, 4 * LANES), jnp.float32),
        ],
        compiler_params=pltpu.CompilerParams(vmem_limit_bytes=40 * 2**20),
        name="windows",
    )(begin_at, band_gain, gathered, padded_taps, visible)
    grid = delays.shape[1]
    block = grid // n
    return pl.pallas_call(
        functools.partial(stack_kernel, n),
        out_shape=jax.ShapeDtypeStruct((block, L), jnp.float32),
        in_specs=[vmem, vmem],
        out_specs=vmem,
        scratch_shapes=[
            pltpu.VMEM((sta * D, L), jnp.bfloat16),
            pltpu.VMEM((2 * block, L), jnp.float32),
            pltpu.VMEM((n - 1, block, L), jnp.bfloat16),
            pltpu.VMEM((n - 1, block, L), jnp.bfloat16),
            pltpu.SemaphoreType.DMA((n - 1,)),
            pltpu.SemaphoreType.DMA((n - 1,)),
        ],
        compiler_params=pltpu.CompilerParams(
            collective_id=0, has_side_effects=True, vmem_limit_bytes=48 * 2**20
        ),
        name="stack",
    )(delays, windows)


def solution(mesh):
    placed = (P("sta", "tile"), P(), P(), P("sta", None), P("sta", "tile"), P("sta", None))
    return jax.shard_map(
        on_device, mesh=mesh, in_specs=placed, out_specs=P(("tile", "sta"), None), check_vma=False
    )
```

```python
import functools
import math

import jax
import jax.numpy as jnp
from jax import lax
from jax.experimental import pallas as pl
from jax.experimental.pallas import tpu as pltpu
from jax.sharding import PartitionSpec as P

TAPS = 64
D = 128
L = 256
WLEN = 384
LANES = 128
CHUNK = 32
EIGHT = jnp.float8_e4m3fn
MESH = pl.DeviceIdType.MESH


def window_kernel(starts_ref, gain_ref, traces_ref, taps_ref, vis_ref, win_ref, unit_ref, padded, held):
    sta, samp = traces_ref.shape
    bands = taps_ref.shape[0]
    padded[:, :LANES] = jnp.zeros((sta, LANES), jnp.float32)
    padded[:, LANES + samp :] = jnp.zeros((sta, LANES), jnp.float32)
    padded[:, LANES : LANES + samp] = traces_ref[...].astype(jnp.float32)

    def take(i, carry):
        for k in range(CHUNK):
            s = i * CHUNK + k
            first = starts_ref[s] + (LANES - TAPS)
            whole = first // LANES
            row = padded[pl.ds(s, 1), pl.ds(pl.multiple_of(whole * LANES, LANES), 5 * LANES)]
            row = pltpu.roll(row, 5 * LANES - (first - whole * LANES), 1)
            held[pl.ds(s, 1), :] = row[:, : 4 * LANES]
        return carry

    lax.fori_loop(0, sta // CHUNK, take, 0)

    tables = []
    for b in range(bands):
        rows = jnp.broadcast_to(taps_ref[b : b + 1, :], (2 * LANES, 2 * LANES))
        table = pltpu.roll(rows, 0, 1, stride=1, stride_axis=0)[:, :LANES]
        high = table.astype(jnp.bfloat16)
        rest = table - high.astype(jnp.float32)
        mid = rest.astype(jnp.bfloat16)
        low = (rest - mid.astype(jnp.float32)).astype(jnp.bfloat16)
        tables.append(jnp.concatenate([low, mid, high], axis=0))
    table = jnp.concatenate(tables, axis=1)
    parts = []
    for j in range(WLEN // LANES):
        x = held[:, j * LANES : (j + 2) * LANES].astype(jnp.bfloat16)
        x = jnp.concatenate([x, x, x], axis=1)
        filtered = jnp.dot(x, table, preferred_element_type=jnp.float32)
        total = None
        for b in range(bands):
            band = filtered[:, b * LANES : (b + 1) * LANES]
            term = band * band * gain_ref[b]
            total = term if total is None else total + term
        parts.append(total.astype(jnp.bfloat16).astype(jnp.float32))
    mean = sum(jnp.sum(part, axis=1, keepdims=True) for part in parts) / WLEN
    vis = vis_ref[...]
    parts = [((part - mean) * vis).astype(jnp.bfloat16).astype(jnp.float32) for part in parts]
    largest = functools.reduce(jnp.maximum, [jnp.max(jnp.abs(part), keepdims=True) for part in parts])
    largest = largest * 2.0**-14
    scale = jnp.full((1, 1), 2.0**-14, jnp.float32)
    unit = jnp.full((1, 1), 2.0**14, jnp.float32)
    for p in (64, 32, 16, 8, 4, 2, 1):
        small = largest * 2.0**p < 256.0
        largest = jnp.where(small, largest * 2.0**p, largest)
        scale = jnp.where(small, scale * 2.0**p, scale)
        unit = jnp.where(small, unit * 2.0**-p, unit)
    unit_ref[...] = unit
    for j, part in enumerate(parts):
        scaled = part * scale
        high = scaled.astype(EIGHT).astype(jnp.float32)
        at = slice(j * LANES, (j + 1) * LANES)
        win_ref[0, :, at] = high
        win_ref[1, :, at] = (scaled - high) * 16.0


def stack_kernel(n, delays_ref, win_ref, unit_ref, out_ref, hankel, total, sent, got, send_sem, recv_sem):
    sta = delays_ref.shape[0]
    block = out_ref.shape[1]
    me = lax.axis_index("sta")
    tile = lax.axis_index("tile")

    barrier = pltpu.get_barrier_semaphore()

    def greet(o, carry):
        pl.semaphore_signal(
            barrier, inc=1, device_id=(lax.rem(me + o, n), tile), device_id_type=MESH
        )
        return carry

    lax.fori_loop(1, n, greet, 0)

    step = 32

    def build(i, carry):
        for k in range(CHUNK // 2):
            s = i * (CHUNK // 2) + k
            at = pl.ds(pl.multiple_of(s * D, D), D)
            for term in range(2):
                rows = jnp.broadcast_to(win_ref[term, pl.ds(s, 1), :], (step, WLEN))
                rows = pltpu.roll(rows, WLEN - (step - 1), 1, stride=1, stride_axis=0)
                rows = rows.astype(EIGHT)
                for m in range(LANES // step):
                    by = LANES - step - m * step
                    moved = pltpu.roll(rows, WLEN - by, 1) if by else rows
                    moved = moved[:, :L].astype(EIGHT)
                    for a in range(L // LANES):
                        first = term * L + a * LANES + m * step
                        hankel[first : first + step, at] = moved[:, a * LANES : (a + 1) * LANES]
        return carry

    lax.fori_loop(0, sta // (CHUNK // 2), build, 0)

    levels = [
        (lax.broadcasted_iota(jnp.int32, (step, block), 0) + k * step).astype(jnp.int8)
        for k in range(D // step)
    ]
    one = jnp.ones((step, block), EIGHT)
    zero = jnp.zeros((step, block), EIGHT)

    unit = unit_ref[...]

    def stack(owner):
        columns = pl.ds(pl.multiple_of(owner * block, block), block)
        total[...] = jnp.zeros_like(total)

        def add(c, carry):
            near = delays_ref[pl.ds(pl.multiple_of(c * CHUNK, CHUNK), CHUNK), columns]
            sums = []
            depth = CHUNK // 2 * D
            for half in range(2):
                pieces = []
                for k in range(half * CHUNK // 2, (half + 1) * CHUNK // 2):
                    row = jnp.broadcast_to(near[k : k + 1, :], (step, block)).astype(jnp.int8)
                    pieces.extend(jnp.where(row == level, one, zero) for level in levels)
                onehot = jnp.concatenate(pieces, axis=0)
                lhs = hankel[:, pl.ds(pl.multiple_of((2 * c + half) * depth, depth), depth)]
                sums.append(jnp.dot(lhs, onehot, preferred_element_type=jnp.float32))
            both = sums[0] + sums[1]
            total[...] += both[:L] + both[L:] * (1.0 / 16.0)
            return carry

        lax.fori_loop(0, sta // CHUNK, add, 0)

    def copy_of(o):
        return pltpu.make_async_remote_copy(
            src_ref=sent.at[o - 1],
            dst_ref=got.at[o - 1],
            send_sem=send_sem.at[o - 1],
            recv_sem=recv_sem.at[o - 1],
            device_id=(lax.rem(me + o, n), tile),
            device_id_type=MESH,
        )

    pl.semaphore_wait(barrier, n - 1)

    def send(o, carry):
        stack(lax.rem(me + o, n))

        @pl.when(o < n)
        def _():
            sent[o - 1] = (total[...] * unit).astype(jnp.bfloat16)
            copy_of(o).start()

        return carry

    lax.fori_loop(1, n + 1, send, 0)
    total[...] *= unit

    def collect(o, carry):
        copy_of(o).wait()
        total[...] += got[o - 1].astype(jnp.float32)
        return carry

    lax.fori_loop(1, n, collect, 0)
    out_ref[...] = total[...] * (1.0 / math.sqrt(sta * n))


def on_device(traces, fir_taps, band_gain, starts, delays, visibility):
    sta = traces.shape[0]
    n = lax.axis_size("sta")
    tile_pos = lax.axis_index("tile")
    gathered = lax.all_gather(traces, "tile", axis=1, tiled=True)
    begin_at = lax.dynamic_index_in_dim(starts, tile_pos, 1, keepdims=False)
    visible = lax.dynamic_index_in_dim(visibility, tile_pos, 1, keepdims=True).astype(jnp.float32)
    padded_taps = jnp.pad(fir_taps, ((0, 0), (2 * LANES - TAPS, 0)))
    samp = gathered.shape[1]
    vmem = pl.BlockSpec(memory_space=pltpu.VMEM)
    smem = pl.BlockSpec(memory_space=pltpu.SMEM)
    windows, unit = pl.pallas_call(
        window_kernel,
        out_shape=[
            jax.ShapeDtypeStruct((2, sta, WLEN), jnp.float32),
            jax.ShapeDtypeStruct((1, 1), jnp.float32),
        ],
        in_specs=[smem, smem, vmem, vmem, vmem],
        out_specs=[vmem, vmem],
        scratch_shapes=[
            pltpu.VMEM((sta, samp + 2 * LANES), jnp.float32),
            pltpu.VMEM((sta, 4 * LANES), jnp.float32),
        ],
        compiler_params=pltpu.CompilerParams(vmem_limit_bytes=40 * 2**20),
        name="windows",
    )(begin_at, band_gain, gathered, padded_taps, visible)
    grid = delays.shape[1]
    block = grid // n
    image = pl.pallas_call(
        functools.partial(stack_kernel, n),
        out_shape=jax.ShapeDtypeStruct((L, block), jnp.float32),
        in_specs=[vmem, vmem, vmem],
        out_specs=vmem,
        scratch_shapes=[
            pltpu.VMEM((2 * L, sta * D), EIGHT),
            pltpu.VMEM((L, block), jnp.float32),
            pltpu.VMEM((n - 1, L, block), jnp.bfloat16),
            pltpu.VMEM((n - 1, L, block), jnp.bfloat16),
            pltpu.SemaphoreType.DMA((n - 1,)),
            pltpu.SemaphoreType.DMA((n - 1,)),
        ],
        compiler_params=pltpu.CompilerParams(
            collective_id=0, has_side_effects=True, vmem_limit_bytes=48 * 2**20
        ),
        name="stack",
    )(delays, windows, unit)
    lagged = jnp.flip(image.reshape(L // LANES, LANES, block), 1).reshape(L, block)
    return lagged.T


def solution(mesh):
    placed = (P("sta", "tile"), P(), P(), P("sta", None), P("sta", "tile"), P("sta", None))
    return jax.shard_map(
        on_device, mesh=mesh, in_specs=placed, out_specs=P(("tile", "sta"), None), check_vma=False
    )
```

```python
import functools
import math

import jax
import jax.numpy as jnp
from jax import lax
from jax.experimental import pallas as pl
from jax.experimental.pallas import tpu as pltpu
from jax.sharding import PartitionSpec as P

TAPS = 64
D = 128
L = 256
WLEN = 384
LANES = 128
CHUNK = 32
MESH = pl.DeviceIdType.MESH


def window_kernel(starts_ref, gain_ref, traces_ref, taps_ref, vis_ref, win_ref, padded, held):
    sta, samp = traces_ref.shape
    bands = taps_ref.shape[0]
    padded[:, :LANES] = jnp.zeros((sta, LANES), jnp.float32)
    padded[:, LANES + samp :] = jnp.zeros((sta, LANES), jnp.float32)
    padded[:, LANES : LANES + samp] = traces_ref[...].astype(jnp.float32)

    def take(i, carry):
        for k in range(CHUNK):
            s = i * CHUNK + k
            first = starts_ref[s] + (LANES - TAPS)
            whole = first // LANES
            row = padded[pl.ds(s, 1), pl.ds(pl.multiple_of(whole * LANES, LANES), 5 * LANES)]
            row = pltpu.roll(row, 5 * LANES - (first - whole * LANES), 1)
            held[pl.ds(s, 1), :] = row[:, : 4 * LANES]
        return carry

    lax.fori_loop(0, sta // CHUNK, take, 0)

    tables = []
    for b in range(bands):
        rows = jnp.broadcast_to(taps_ref[b : b + 1, :], (2 * LANES, 2 * LANES))
        table = pltpu.roll(rows, 0, 1, stride=1, stride_axis=0)[:, :LANES]
        high = table.astype(jnp.bfloat16)
        rest = table - high.astype(jnp.float32)
        mid = rest.astype(jnp.bfloat16)
        low = (rest - mid.astype(jnp.float32)).astype(jnp.bfloat16)
        tables.append(jnp.concatenate([low, mid, high], axis=0))
    table = jnp.concatenate(tables, axis=1)
    parts = []
    for j in range(WLEN // LANES):
        x = held[:, j * LANES : (j + 2) * LANES].astype(jnp.bfloat16)
        x = jnp.concatenate([x, x, x], axis=1)
        filtered = jnp.dot(x, table, preferred_element_type=jnp.float32)
        total = None
        for b in range(bands):
            band = filtered[:, b * LANES : (b + 1) * LANES]
            term = band * band * gain_ref[b]
            total = term if total is None else total + term
        parts.append(total.astype(jnp.bfloat16).astype(jnp.float32))
    mean = sum(jnp.sum(part, axis=1, keepdims=True) for part in parts) / WLEN
    vis = vis_ref[...]
    for j, part in enumerate(parts):
        out = ((part - mean) * vis).astype(jnp.bfloat16)
        win_ref[:, j * LANES : (j + 1) * LANES] = out.astype(jnp.float32)


def stack_kernel(n, delays_ref, win_ref, out_ref, hankel, total, sent, got, send_sem, recv_sem):
    sta = delays_ref.shape[0]
    block = out_ref.shape[1]
    me = lax.axis_index("sta")
    tile = lax.axis_index("tile")

    barrier = pltpu.get_barrier_semaphore()

    def greet(o, carry):
        pl.semaphore_signal(
            barrier, inc=1, device_id=(lax.rem(me + o, n), tile), device_id_type=MESH
        )
        return carry

    lax.fori_loop(1, n, greet, 0)

    step = 16
    lane = lax.broadcasted_iota(jnp.int32, (step, LANES), 1)

    def build(i, carry):
        for k in range(CHUNK):
            s = i * CHUNK + k
            rows = jnp.broadcast_to(win_ref[pl.ds(s, 1), :], (step, WLEN))
            rows = pltpu.roll(rows, WLEN - (step - 1), 1, stride=1, stride_axis=0)
            rows = rows.astype(jnp.bfloat16)
            at = pl.ds(pl.multiple_of(s * D, D), D)
            for m in range(LANES // step):
                by = LANES - step - m * step
                moved = [rows[:, c * LANES : (c + 1) * LANES] for c in range(WLEN // LANES)]
                if by:
                    moved = [pltpu.roll(part, LANES - by, 1) for part in moved]
                for a in range(L // LANES):
                    first = a * LANES + m * step
                    part = moved[a]
                    if by:
                        part = jnp.where(lane < LANES - by, part, moved[a + 1])
                    hankel[first : first + step, at] = part
        return carry

    lax.fori_loop(0, sta // CHUNK, build, 0)

    levels = [
        (lax.broadcasted_iota(jnp.int32, (step, block), 0) + k * step)
        .astype(jnp.float32)
        .astype(jnp.bfloat16)
        for k in range(D // step)
    ]
    one = jnp.ones((step, block), jnp.bfloat16)
    zero = jnp.zeros((step, block), jnp.bfloat16)

    def stack(owner):
        columns = pl.ds(pl.multiple_of(owner * block, block), block)
        total[...] = jnp.zeros_like(total)

        def add(c, carry):
            near = delays_ref[pl.ds(pl.multiple_of(c * CHUNK, CHUNK), CHUNK), columns].astype(
                jnp.float32
            )
            sums = []
            depth = CHUNK // 2 * D
            for half in range(2):
                pieces = []
                for k in range(half * CHUNK // 2, (half + 1) * CHUNK // 2):
                    row = jnp.broadcast_to(near[k : k + 1, :], (step, block)).astype(jnp.bfloat16)
                    pieces.extend(jnp.where(row == level, one, zero) for level in levels)
                onehot = jnp.concatenate(pieces, axis=0)
                lhs = hankel[:, pl.ds(pl.multiple_of((2 * c + half) * depth, depth), depth)]
                sums.append(jnp.dot(lhs, onehot, preferred_element_type=jnp.float32))
            total[...] += sums[0] + sums[1]
            return carry

        lax.fori_loop(0, sta // CHUNK, add, 0)

    def copy_of(o):
        return pltpu.make_async_remote_copy(
            src_ref=sent.at[o - 1],
            dst_ref=got.at[o - 1],
            send_sem=send_sem.at[o - 1],
            recv_sem=recv_sem.at[o - 1],
            device_id=(lax.rem(me + o, n), tile),
            device_id_type=MESH,
        )

    pl.semaphore_wait(barrier, n - 1)

    def send(o, carry):
        stack(lax.rem(me + o, n))

        @pl.when(o < n)
        def _():
            sent[o - 1] = total[...].astype(jnp.bfloat16)
            copy_of(o).start()

        return carry

    lax.fori_loop(1, n + 1, send, 0)

    def collect(o, carry):
        copy_of(o).wait()
        total[...] += got[o - 1].astype(jnp.float32)
        return carry

    lax.fori_loop(1, n, collect, 0)
    out_ref[...] = total[...] * (1.0 / math.sqrt(sta * n))


def on_device(traces, fir_taps, band_gain, starts, delays, visibility):
    sta = traces.shape[0]
    n = lax.axis_size("sta")
    tile_pos = lax.axis_index("tile")
    gathered = lax.all_gather(traces, "tile", axis=1, tiled=True)
    begin_at = lax.dynamic_index_in_dim(starts, tile_pos, 1, keepdims=False)
    visible = lax.dynamic_index_in_dim(visibility, tile_pos, 1, keepdims=True).astype(jnp.float32)
    padded_taps = jnp.pad(fir_taps, ((0, 0), (2 * LANES - TAPS, 0)))
    samp = gathered.shape[1]
    vmem = pl.BlockSpec(memory_space=pltpu.VMEM)
    smem = pl.BlockSpec(memory_space=pltpu.SMEM)
    windows = pl.pallas_call(
        window_kernel,
        out_shape=jax.ShapeDtypeStruct((sta, WLEN), jnp.float32),
        in_specs=[smem, smem, vmem, vmem, vmem],
        out_specs=vmem,
        scratch_shapes=[
            pltpu.VMEM((sta, samp + 2 * LANES), jnp.float32),
            pltpu.VMEM((sta, 4 * LANES), jnp.float32),
        ],
        compiler_params=pltpu.CompilerParams(vmem_limit_bytes=40 * 2**20),
        name="windows",
    )(begin_at, band_gain, gathered, padded_taps, visible)
    grid = delays.shape[1]
    block = grid // n
    image = pl.pallas_call(
        functools.partial(stack_kernel, n),
        out_shape=jax.ShapeDtypeStruct((L, block), jnp.float32),
        in_specs=[vmem, vmem],
        out_specs=vmem,
        scratch_shapes=[
            pltpu.VMEM((L, sta * D), jnp.bfloat16),
            pltpu.VMEM((L, block), jnp.float32),
            pltpu.VMEM((n - 1, L, block), jnp.bfloat16),
            pltpu.VMEM((n - 1, L, block), jnp.bfloat16),
            pltpu.SemaphoreType.DMA((n - 1,)),
            pltpu.SemaphoreType.DMA((n - 1,)),
        ],
        compiler_params=pltpu.CompilerParams(
            collective_id=0, has_side_effects=True, vmem_limit_bytes=48 * 2**20
        ),
        name="stack",
    )(delays, windows)
    lagged = jnp.flip(image.reshape(L // LANES, LANES, block), 1).reshape(L, block)
    return lagged.T


def solution(mesh):
    placed = (P("sta", "tile"), P(), P(), P("sta", None), P("sta", "tile"), P("sta", None))
    return jax.shard_map(
        on_device, mesh=mesh, in_specs=placed, out_specs=P(("tile", "sta"), None), check_vma=False
    )
```
